32 devices in a mesh: ctx: 16 (over z, x, core), exp: 2 (over y).
Axes of the slice: x: 2, y: 2, z: 4, core: 2. Of those that a mesh axis runs over, the one named last changes fastest.
Arguments:
- hidden_acts: bfloat16 [32, 16, 32, 2048], P('ctx', None, None, 'exp'), may hold values from -6 to 6
- down_weight: bfloat16 [32, 2048, 2880], P('ctx', 'exp'), may hold values from -0.125 to 0.125
- expert_ids: int32 [2048, 4], P('ctx'), may hold values from 0 to 31, all different within a row; in each aligned block of 128 rows (0 to 127, 128 to 255, ...) at most 32 rows name the same one
- route_logits: float32 [2048, 4], P('ctx'), may hold values from -4 to 4
- out_grad: bfloat16 [2048, 2880], P('ctx', 'exp'), may hold values from -6 to 6
Outputs:
- combined: bfloat16 [2048, 2880], P('ctx', 'exp')
- grad_logits: float32 [2048, 4], P('ctx')
- grad_hidden: bfloat16 [32, 16, 32, 2048], P('ctx', None, None, 'exp')
- grad_weight: bfloat16 [32, 2048, 2880], P('ctx', 'exp')
The draws below stay inside these ranges and needn't reach their ends.
Inputs may be any that keep to these rules, and one draw needn't show every extreme that they name: `expert_ids`: each token names 4 different experts; within each aligned block of 128 tokens no expert is named by more than 32 tokens, a bound that some block reaches.
All inputs are finite; a program needn't handle non-finite values.
Results may differ from the reference program's by a relative error of at most 0.014.
Values may be sent and summed in bfloat16 or wider, within the bound.
A program may use at most 128 MiB of HBM per device.

```python
import math
import jax
import jax.numpy as jnp
import numpy as np
from jax import lax

D = 2880
TOP = 4
HID = 2048
TOK_DEV = 128
EXPERTS = 32
CAP = 32
SEQ_LEN = 2048
N_CTX = 16
N_EXP = 2


def shard_levels(stream_key, shape, cuts, least, largest):
    loudness, own = 1.0, jax.random.fold_in(stream_key, 6)
    for axis_at, blocks in cuts:
        draws = jnp.exp(jax.random.uniform(jax.random.fold_in(own, axis_at), (blocks,), jnp.float32, least / len(cuts), largest / len(cuts)))
        loudness = loudness * jnp.repeat(draws, shape[axis_at] // blocks).reshape([-1 if axis == axis_at else 1 for axis in range(len(shape))])
    return loudness


def shared_out(stream_key, own, number, rows, count, top, bound, slope):
    sequence = jax.random.permutation(stream_key, count)
    packed, common = portions_of(count, rows * top, bound, slope, True), portions_of(count, rows * top, bound, slope, False)
    places = jnp.arange(count)

    def named(tallies, rotation):
        used = int((tallies > 0).sum())
        fixed = max(1, used // 4)
        passed = fixed + (places - fixed + rotation * (used - fixed)) % max(1, count - fixed)
        return jnp.zeros((count,), jnp.int32).at[sequence[jnp.where(places < fixed, places, passed)]].set(jnp.asarray(tallies, jnp.int32))

    tallies = jnp.where(number % 4 == 0, named(packed, number // 4), named(common, number - number // 4 - 1))
    mixed = jax.random.permutation(jax.random.fold_in(own, 3), count)
    giver, sink = mixed[0:count // 2 * 2:2], mixed[1:count // 2 * 2:2]
    room = jnp.minimum(tallies[giver] - 1, bound - tallies[sink]) // 2
    room = jnp.where((giver == sequence[0]) | (sink == sequence[0]) | (tallies[sink] == 0), 0, jnp.maximum(room, 0))
    passed = jax.random.randint(jax.random.fold_in(own, 4), (count // 2,), 0, 1 << 20) % (room + 1)
    tallies = tallies.at[giver].add(-passed).at[sink].add(passed)
    items = jnp.searchsorted(jnp.cumsum(tallies), jnp.arange(rows * top), side="right").astype(jnp.int32)
    table = items.reshape(top, rows).T
    table = table[jax.random.permutation(jax.random.fold_in(own, 1), rows)]
    rotation = jax.random.randint(jax.random.fold_in(own, 2), (rows, 1), 0, top)
    return jnp.take_along_axis(table, (jnp.arange(top)[None, :] + rotation) % top, axis=1)


def portions_of(count, total, most, slope, full):
    weights = [(1 << 20) // math.isqrt(grade ** slope) + 1 for grade in range(1, count + 1)]
    largest = most if full else min(most, max(-(-total // count), total * weights[0] // sum(weights)))
    least = 1 if total - largest >= count - 1 else 0
    given, spare = [largest] + [least] * (count - 1), total - largest - least * (count - 1)
    while spare > 0:
        candidates = [i for i in range(1, count) if given[i] < largest] or [i for i in range(1, count) if given[i] < most]
        mass, budget = sum([weights[i] for i in candidates]), spare
        for i in candidates:
            extra = min(most - given[i], max(1, budget * weights[i] // mass), spare)
            given[i] = given[i] + extra
            spare = spare - extra
    return np.array(given)


def bell_draw(key, extent, width, limit, split=(), kind=jnp.bfloat16):
    entries = jax.random.normal(key, extent, jnp.float32) * width
    if len(split) > 0:
        entries = shard_levels(key, extent, split, -0.22, 0.18) * entries
    return jnp.clip(entries, min=-limit, max=limit).astype(kind)


def setup_inputs(seed: int = 0) -> dict:
    key_list = jax.random.split(jax.random.key(seed), 6)
    hidden_acts = bell_draw(key_list[0], (EXPERTS, N_CTX, CAP, HID), 1.0, 6.0, ((0, 16), (3, 2)))
    down_weight = bell_draw(key_list[1], (EXPERTS, HID, D), HID ** -0.5, 0.125, ((0, 16), (1, 2)))
    expert_ids_keys = jax.random.split(jax.random.fold_in(key_list[2], 1), SEQ_LEN // TOK_DEV)
    expert_ids_turns = jax.random.permutation(jax.random.fold_in(key_list[2], 3), SEQ_LEN // TOK_DEV)
    expert_ids = jax.vmap(lambda own, number: shared_out(jax.random.fold_in(key_list[2], 2), own, number, TOK_DEV, EXPERTS, TOP, CAP, 1))(expert_ids_keys, expert_ids_turns).reshape((SEQ_LEN, TOP))
    route_logits = bell_draw(key_list[3], (SEQ_LEN, TOP), 1.0, 4.0, ((0, 16),), jnp.float32)
    out_grad = bell_draw(key_list[4], (SEQ_LEN, D), 1.0, 6.0, ((0, 16), (1, 2)))
    return dict(hidden_acts=hidden_acts, down_weight=down_weight, expert_ids=expert_ids, route_logits=route_logits, out_grad=out_grad)


def slot_index(group_ids, expert_count):
    onehot = (group_ids[..., None] == jnp.arange(expert_count, dtype=jnp.int32)).astype(jnp.int32)
    running = jnp.cumsum(onehot, axis=1)
    return (jnp.sum(running * onehot, axis=2) - 1).astype(jnp.int32)


def reference(hidden_acts, down_weight, expert_ids, route_logits, out_grad):
    weights = jnp.exp(route_logits)
    route_probs = weights / jnp.sum(weights, axis=1, keepdims=True)
    slot_pos = slot_index(expert_ids.reshape(N_CTX, TOK_DEV * TOP), EXPERTS).reshape(SEQ_LEN, TOP)
    group_of = (jnp.arange(SEQ_LEN, dtype=jnp.int32) // TOK_DEV)[:, None]
    flat_index = ((expert_ids * N_CTX + group_of) * CAP + slot_pos).reshape(-1).astype(jnp.int32)
    block_width = HID // N_EXP

    def expert_rows(operands):
        activations, weight = operands
        act_rows = activations.reshape(N_CTX * CAP, HID)
        running_sum = jnp.zeros((N_CTX * CAP, D), jnp.float32)
        for part_index in range(N_EXP):
            first_col = part_index * block_width
            block_out = jnp.dot(act_rows[:, first_col:first_col + block_width], weight[first_col:first_col + block_width], preferred_element_type=jnp.float32).astype(jnp.bfloat16)
            running_sum = running_sum + lax.optimization_barrier(block_out).astype(jnp.float32)
        return running_sum

    expert_out = lax.map(expert_rows, (hidden_acts, down_weight))
    picked = expert_out.reshape(-1, D)[flat_index].reshape(SEQ_LEN, TOP, D)
    combined = jnp.einsum("tk,tkd->td", route_probs, picked).astype(jnp.bfloat16)
    grad_values = out_grad.astype(jnp.float32)
    prob_grad = jnp.einsum("td,tkd->tk", grad_values, picked)
    grad_logits = route_probs * (prob_grad - jnp.sum(route_probs * prob_grad, axis=1, keepdims=True))
    slot_rows = (route_probs[:, :, None] * grad_values[:, None, :]).astype(jnp.bfloat16).reshape(-1, D)
    slot_grad = jnp.zeros((EXPERTS * N_CTX * CAP, D), jnp.bfloat16).at[flat_index].set(slot_rows).reshape(EXPERTS, N_CTX * CAP, D)

    def expert_grads(operands):
        activations, weight, grad_rows = operands
        act_rows = activations.reshape(N_CTX * CAP, HID)
        grad_acts = jnp.dot(grad_rows, weight.T, preferred_element_type=jnp.float32).astype(jnp.bfloat16).reshape(N_CTX, CAP, HID)
        grad_w = jnp.dot(act_rows.T, grad_rows, preferred_element_type=jnp.float32).astype(jnp.bfloat16)
        return grad_acts, grad_w

    grad_hidden, grad_weight = lax.map(expert_grads, (hidden_acts, down_weight, slot_grad))
    return (combined, grad_logits, grad_hidden, grad_weight)
```

```python
import jax
import jax.numpy as jnp
from jax import lax
from jax.sharding import PartitionSpec as P

AXES = ("ctx", "exp")


def local(hidden_acts, down_weight, expert_ids, route_logits, out_grad):
    local_experts, groups, capacity, _ = hidden_acts.shape
    tok_rows, top_count = expert_ids.shape
    width = out_grad.shape[1]
    parts = lax.axis_size("exp")
    first = lax.axis_index("ctx") * local_experts

    weights = jnp.exp(route_logits)
    route_probs = weights / jnp.sum(weights, axis=1, keepdims=True)

    full_grad = lax.all_gather(out_grad, AXES).reshape(groups, parts, tok_rows, width)
    routes = lax.all_gather(
        jnp.concatenate([expert_ids.astype(jnp.float32), route_probs], axis=1).T, "ctx"
    )
    ids = routes[:, :top_count].astype(jnp.int32)
    probs = routes[:, top_count:]

    mine = first + jnp.arange(local_experts, dtype=jnp.int32)
    named = ids[None] == mine[:, None, None, None]
    taken = jnp.any(named, axis=2)
    prob_of = jnp.sum(jnp.where(named, probs[None], 0.0), axis=2)
    order = jnp.arange(tok_rows)
    earlier = (order[:, None] < order[None, :]).astype(jnp.bfloat16)
    position = jnp.einsum(
        "ect,tu->ecu", taken.astype(jnp.bfloat16), earlier, preferred_element_type=jnp.float32
    ).astype(jnp.int32)
    slots = jnp.arange(capacity, dtype=jnp.int32)
    holds = taken[:, :, None, :] & (position[:, :, None, :] == slots[:, None])
    select = holds.astype(jnp.bfloat16)
    slot_prob = jnp.sum(jnp.where(holds, prob_of[:, :, None, :], 0.0), axis=3)

    rows = (
        jnp.einsum(
            "escj,ejd->escd", hidden_acts, down_weight, preferred_element_type=jnp.float32
        )
        * slot_prob[..., None]
    ).astype(jnp.bfloat16)
    mixed = jnp.stack(
        [
            jnp.einsum(
                "ecst,ecsd->ctd",
                select,
                rows[..., part * width : (part + 1) * width],
                preferred_element_type=jnp.float32,
            ).astype(jnp.bfloat16)
            for part in range(parts)
        ],
        axis=1,
    )
    combined = lax.psum_scatter(
        mixed.reshape(groups * parts, tok_rows, width), AXES, scatter_dimension=0
    )

    slot_grad = jnp.concatenate(
        [
            (
                jnp.einsum(
                    "ecst,ctd->ecsd",
                    select,
                    full_grad[:, part],
                    preferred_element_type=jnp.float32,
                )
                * slot_prob[..., None]
            ).astype(jnp.bfloat16)
            for part in range(parts)
        ],
        axis=3,
    )
    grad_acts = jnp.einsum(
        "escd,ejd->escj", slot_grad, down_weight, preferred_element_type=jnp.float32
    )
    grad_hidden = grad_acts.astype(jnp.bfloat16)
    slot_sum = jnp.sum(grad_acts * hidden_acts.astype(jnp.float32), axis=3)
    token_sum = jnp.sum(jnp.where(holds, slot_sum[..., None], 0.0), axis=2)
    route_sum = jnp.sum(jnp.where(named, token_sum[:, :, None, :], 0.0), axis=0)
    route_sum = lax.psum(lax.psum_scatter(route_sum, "ctx", scatter_dimension=0), "exp").T
    grad_logits = route_sum - route_probs * jnp.sum(route_sum, axis=1, keepdims=True)
    grad_weight = jnp.einsum(
        "escj,escd->ejd", hidden_acts, slot_grad, preferred_element_type=jnp.float32
    ).astype(jnp.bfloat16)
    return (combined, grad_logits, grad_hidden, grad_weight)


def solution(mesh):
    placed = (
        P("ctx", None, None, "exp"),
        P("ctx", "exp", None),
        P("ctx", None),
        P("ctx", None),
        P("ctx", "exp"),
    )
    return jax.shard_map(
        local,
        mesh=mesh,
        in_specs=placed,
        out_specs=(
            P("ctx", "exp"),
            P("ctx", None),
            P("ctx", None, None, "exp"),
            P("ctx", "exp", None),
        ),
        check_vma=False,
    )
```

```python
import functools

import jax
import jax.numpy as jnp
from jax import lax
from jax.experimental import pallas as pl
from jax.experimental.pallas import tpu as pltpu
from jax.sharding import PartitionSpec as P

MESH = pl.DeviceIdType.MESH
PAIR = 2
F32 = jnp.float32
BF16 = jnp.bfloat16


def exchange_kernel(
    outer,
    parts,
    acts_ref,
    weight_ref,
    prob_ref,
    back_ref,
    grad_ref,
    full_ref,
    combined_ref,
    weight_v,
    rows_v,
    away_v,
    home_v,
    core_v,
    far0_v,
    far1_v,
    near0_v,
    near1_v,
    last_v,
    load_sem,
    az_s,
    az_r,
    au_s,
    au_r,
    av_s,
    av_r,
    ac_s,
    ac_r,
    rc_s,
    rc_r,
    rv_s,
    rv_r,
    ru_s,
    ru_r,
    rz_s,
    rz_r,
):
    ctx, y = lax.axis_index("ctx"), lax.axis_index("exp")
    z, x, c = ctx // (PAIR * PAIR), (ctx // PAIR) % PAIR, ctx % PAIR
    experts, capacity = rows_v.shape[1], rows_v.shape[2]
    tokens, width = grad_ref.shape
    half = tokens // 2
    spans = (pl.ds(0, half), pl.ds(half, half))

    def at_z(k):
        return (((z + k) % outer) * (PAIR * PAIR) + x * PAIR + c, y)

    def at_x(k):
        return (z * (PAIR * PAIR) + ((x + k) % PAIR) * PAIR + c, y)

    def at_y(k):
        return (ctx, (y + k) % parts)

    sibling = (z * (PAIR * PAIR) + x * PAIR + (1 - c), y)
    mid_to, mid_n = (at_x, at_y), (PAIR, parts)
    end_to, end_n = (at_y, at_x), (parts, PAIR)

    def send(src, dst, s, r, to):
        return pltpu.make_async_remote_copy(
            src_ref=src, dst_ref=dst, send_sem=s, recv_sem=r, device_id=to, device_id_type=MESH
        )

    loads = [
        pltpu.make_async_copy(weight_ref.at[e], weight_v.at[e], load_sem.at[e])
        for e in range(experts)
    ]
    for load in loads:
        load.start()
    own = pltpu.make_async_copy(grad_ref, full_ref.at[z, x, c, y], load_sem.at[experts])
    own.start()

    barrier = pltpu.get_barrier_semaphore()
    peers = [at_z(k) for k in range(1, outer)]
    peers += [at_x(k) for k in range(1, PAIR)]
    peers += [at_y(k) for k in range(1, parts)]
    peers += [sibling]
    for peer in peers:
        pl.semaphore_signal(barrier, inc=1, device_id=peer, device_id_type=MESH)
    pl.semaphore_wait(barrier, len(peers))

    def from_z(k):
        return (z - k + outer) % outer

    def gz(h, k):
        place = full_ref.at[z, x, c, y, spans[h]]
        return send(grad_ref.at[spans[h]], place, az_s.at[h, k], az_r.at[h, k], at_z(k))

    def gu(h, k, j):
        place = full_ref.at[from_z(k), x, c, y, spans[h]]
        return send(place, place, au_s.at[h, k, j], au_r.at[h, k, j], mid_to[h](j))

    def gv(h, k, j):
        if h == 0:
            place = full_ref.at[from_z(k), :, c, y, spans[h]]
        else:
            place = full_ref.at[from_z(k), x, c, :, spans[h]]
        return send(place, place, av_s.at[h, k, j], av_r.at[h, k, j], end_to[h](j))

    def gc(h, k):
        place = full_ref.at[from_z(k), :, c, :, spans[h]]
        return send(place, place, ac_s.at[h, k], ac_r.at[h, k], sibling)

    for k in range(1, outer):
        for h in range(2):
            gz(h, k).start()
    own.wait()

    def gather_mid(k):
        for h in range(2):
            if k:
                gz(h, k).wait_recv()
            for j in range(1, mid_n[h]):
                gu(h, k, j).start()

    def gather_end(k):
        for h in range(2):
            for j in range(1, mid_n[h]):
                gu(h, k, j).wait_recv()
            for j in range(1, end_n[h]):
                gv(h, k, j).start()

    def gather_core(k):
        for h in range(2):
            for j in range(1, end_n[h]):
                gv(h, k, j).wait_recv()
            gc(h, k).start()

    gather_mid(0)

    block = acts_ref.shape[1] // 2
    groups = block // capacity

    def product(e, m):
        start = pl.multiple_of(m * block, block)
        value = jnp.dot(
            acts_ref[e, pl.ds(start, block), :], weight_v[e], preferred_element_type=F32
        )
        value = (value * prob_ref[e, pl.ds(start, block), :]).astype(BF16)
        rows_v[pl.ds(m * groups, groups), e] = value.reshape(groups, capacity, value.shape[1])

    for e in range(experts):
        loads[e].wait()
        if e == 0:
            gather_end(0)
        else:
            for k in range(1, outer):
                gather_mid(k)
        lax.fori_loop(0, 2, lambda m, _: (product(e, m), 0)[1], 0)

    for k in range(1, outer):
        gather_end(k)

    order = list(range(1, outer)) + [0]

    def rc(i):
        zi = (z + order[i]) % outer
        return send(away_v.at[i % 2], core_v.at[zi], rc_s.at[i], rc_r.at[i], sibling)

    def rv(h, i, j):
        zi = (z + order[i]) % outer
        if h == 0:
            src, dst = home_v.at[zi, :, (y + j) % parts, spans[0]], far0_v.at[zi, j - 1]
        else:
            src, dst = home_v.at[zi, (x + j) % PAIR, :, spans[1]], far1_v.at[zi, j - 1]
        return send(src, dst, rv_s.at[h, i, j], rv_r.at[h, i, j], end_to[h](j))

    def ru(h, i, j):
        zi = (z + order[i]) % outer
        if h == 0:
            src, dst = far0_v.at[zi, 0, (x + j) % PAIR], near0_v.at[zi, j - 1]
        else:
            src, dst = far1_v.at[zi, 0, (y + j) % parts], near1_v.at[zi, j - 1]
        return send(src, dst, ru_s.at[h, i, j], ru_r.at[h, i, j], mid_to[h](j))

    near = (near0_v, near1_v)

    def rz(h, k):
        zi = (z + k) % outer
        return send(near[h].at[zi, 0], last_v.at[h, k - 1], rz_s.at[h, k], rz_r.at[h, k], at_z(k))

    def mix(zi, xi, ci, put):
        group = zi * (PAIR * PAIR) + xi * PAIR + ci
        value = jnp.dot(
            back_ref[group],
            rows_v[group].reshape(experts * capacity, rows_v.shape[3]),
            preferred_element_type=F32,
        ).astype(BF16)
        for part in range(parts):
            put(xi, part, value[:, part * width : (part + 1) * width])

    for i in range(outer):
        zi = (z + order[i]) % outer
        if i >= 2:
            rc(i - 2).wait_send()

        def put_away(xi, part, value):
            away_v[i % 2, xi, part] = value

        def put_home(xi, part, value):
            home_v[zi, xi, part] = value

        lax.fori_loop(0, PAIR, lambda xi, _: (mix(zi, xi, 1 - c, put_away), 0)[1], 0)
        rc(i).start()
        lax.fori_loop(0, PAIR, lambda xi, _: (mix(zi, xi, c, put_home), 0)[1], 0)
        gather_core(i)

    def add(first, others):
        total = first.astype(F32)
        for other in others:
            total = total + other.astype(F32)
        return total.astype(BF16)

    def sum_core(i):
        zi = (z + order[i]) % outer
        rc(i).wait_recv()

        def step(n, _):
            xi, part = n // parts, n % parts
            home_v[zi, xi, part] = add(home_v[zi, xi, part], [core_v[zi, xi, part]])
            return 0

        lax.fori_loop(0, PAIR * parts, step, 0)
        for h in range(2):
            for j in range(1, end_n[h]):
                rv(h, i, j).start()

    def sum_end(i):
        zi = (z + order[i]) % outer
        for h in range(2):
            for j in range(1, end_n[h]):
                rv(h, i, j).wait_recv()
        for xi in range(PAIR):
            others = [far0_v[zi, j - 1, xi] for j in range(1, end_n[0])]
            far0_v[zi, 0, xi] = add(home_v[zi, xi, y, spans[0]], others)
        for part in range(parts):
            others = [far1_v[zi, j - 1, part] for j in range(1, end_n[1])]
            far1_v[zi, 0, part] = add(home_v[zi, x, part, spans[1]], others)
        for h in range(2):
            for j in range(1, mid_n[h]):
                ru(h, i, j).start()

    def sum_mid(i):
        zi = (z + order[i]) % outer
        for h in range(2):
            for j in range(1, mid_n[h]):
                ru(h, i, j).wait_recv()
            others = [near[h][zi, j - 1] for j in range(1, mid_n[h])]
            mine = far0_v[zi, 0, x] if h == 0 else far1_v[zi, 0, y]
            near[h][zi, 0] = add(mine, others)
            if order[i]:
                rz(h, order[i]).start()

    sum_core(0)
    for i in range(outer):
        if i + 1 < outer:
            sum_core(i + 1)
        sum_end(i)
        if i:
            sum_mid(i - 1)
    sum_mid(outer - 1)

    for h in range(2):
        for k in range(1, outer):
            rz(h, k).wait_recv()
        combined_ref[spans[h], :] = add(
            near[h][z, 0], [last_v[h, k - 1] for k in range(1, outer)]
        )

    for h in range(2):
        for k in range(outer):
            if k:
                gz(h, k).wait_send()
                rz(h, k).wait_send()
            for j in range(1, mid_n[h]):
                gu(h, k, j).wait_send()
                ru(h, k, j).wait_send()
            for j in range(1, end_n[h]):
                gv(h, k, j).wait_send()
                rv(h, k, j).wait_send()
            gc(h, k).wait()
    for i in range(max(0, outer - 2), outer):
        rc(i).wait_send()


def exchange(acts, weight, slot_prob, back, out_grad, outer, parts):
    experts, slots, _ = acts.shape
    groups = outer * PAIR * PAIR
    capacity = slots // groups
    tokens, width = out_grad.shape
    full = parts * width
    half = tokens // 2
    vmem = pl.BlockSpec(memory_space=pltpu.VMEM)
    hbm = pl.BlockSpec(memory_space=pl.ANY)
    dma = pltpu.SemaphoreType.DMA
    most = max(PAIR, parts)
    pairs = [(2, outer), (2, outer, most), (2, outer, most), (2, outer)]
    pairs += [(outer,), (2, outer, most), (2, outer, most), (2, outer)]
    sems = [dma((experts + 1,))]
    for shape in pairs:
        sems += [dma(shape), dma(shape)]
    return pl.pallas_call(
        functools.partial(exchange_kernel, outer, parts),
        out_shape=(
            jax.ShapeDtypeStruct((outer, PAIR, PAIR, parts, tokens, width), BF16),
            jax.ShapeDtypeStruct((tokens, width), BF16),
        ),
        in_specs=[vmem, hbm, vmem, vmem, hbm],
        out_specs=(hbm, vmem),
        scratch_shapes=[
            pltpu.VMEM(weight.shape, BF16),
            pltpu.VMEM((groups, experts, capacity, full), BF16),
            pltpu.VMEM((2, PAIR, parts, tokens, width), BF16),
            pltpu.VMEM((outer, PAIR, parts, tokens, width), BF16),
            pltpu.VMEM((outer, PAIR, parts, tokens, width), BF16),
            pltpu.VMEM((outer, parts - 1, PAIR, half, width), BF16),
            pltpu.VMEM((outer, PAIR - 1, parts, half, width), BF16),
            pltpu.VMEM((outer, PAIR - 1, half, width), BF16),
            pltpu.VMEM((outer, parts - 1, half, width), BF16),
            pltpu.VMEM((2, outer - 1, half, width), BF16),
        ]
        + sems,
        compiler_params=pltpu.CompilerParams(
            collective_id=0, has_side_effects=True, vmem_limit_bytes=62 * 1024 * 1024
        ),
        cost_estimate=pl.CostEstimate(
            flops=2 * experts * slots * weight.shape[1] * full,
            bytes_accessed=4 * weight.size,
            transcendentals=0,
        ),
    )(acts, weight, slot_prob, back, out_grad)


def slots_kernel(select_ref, prob_ref, full_ref, out_ref):
    experts, _, capacity, _ = out_ref.shape
    parts, _, width = full_ref.shape[1:]
    for part in range(parts):
        value = jnp.dot(select_ref[0], full_ref[0, part], preferred_element_type=F32)
        value = (value * prob_ref[0]).astype(BF16).reshape(experts, capacity, width)
        out_ref[:, 0, :, part * width : (part + 1) * width] = value


def spread(select, slot_prob, full_grad, experts):
    groups, both, tokens = select.shape
    _, parts, _, width = full_grad.shape
    capacity = both // experts
    return pl.pallas_call(
        slots_kernel,
        grid=(groups,),
        out_shape=jax.ShapeDtypeStruct((experts, groups, capacity, parts * width), BF16),
        in_specs=[
            pl.BlockSpec((1, both, tokens), lambda g: (g, 0, 0)),
            pl.BlockSpec((1, both, 1), lambda g: (g, 0, 0)),
            pl.BlockSpec((1, parts, tokens, width), lambda g: (g, 0, 0, 0)),
        ],
        out_specs=pl.BlockSpec((experts, 1, capacity, parts * width), lambda g: (0, g, 0, 0)),
        compiler_params=pltpu.CompilerParams(vmem_limit_bytes=32 * 1024 * 1024),
    )(select, slot_prob, full_grad)


def local(hidden_acts, down_weight, expert_ids, route_logits, out_grad):
    local_experts, groups, capacity, hidden = hidden_acts.shape
    tok_rows, top_count = expert_ids.shape
    width = out_grad.shape[1]
    parts = lax.axis_size("exp")
    first = lax.axis_index("ctx") * local_experts

    weights = jnp.exp(route_logits)
    route_probs = weights / jnp.sum(weights, axis=1, keepdims=True)

    routes = lax.all_gather(
        jnp.concatenate([expert_ids.astype(F32), route_probs], axis=1).T, "ctx"
    )
    ids = routes[:, :top_count].astype(jnp.int32)
    probs = routes[:, top_count:]

    mine = first + jnp.arange(local_experts, dtype=jnp.int32)
    named = ids[:, None] == mine[None, :, None, None]
    taken = jnp.any(named, axis=2)
    prob_of = jnp.sum(jnp.where(named, probs[:, None], 0.0), axis=2)
    order = jnp.arange(tok_rows)
    earlier = (order[:, None] < order[None, :]).astype(BF16)
    position = jnp.einsum(
        "cet,tu->ceu", taken.astype(BF16), earlier, preferred_element_type=F32
    ).astype(jnp.int32)
    slots = jnp.arange(capacity, dtype=jnp.int32)
    holds = taken[:, :, None, :] & (position[:, :, None, :] == slots[:, None])
    slot_prob = jnp.sum(jnp.where(holds, prob_of[:, :, None, :], 0.0), axis=3)
    select = holds.astype(BF16).reshape(groups, local_experts * capacity, tok_rows)
    back = select.swapaxes(1, 2)

    full_grad, combined = exchange(
        hidden_acts.reshape(local_experts, groups * capacity, hidden),
        down_weight,
        slot_prob.swapaxes(0, 1).reshape(local_experts, groups * capacity, 1),
        back,
        out_grad,
        groups // (PAIR * PAIR),
        parts,
    )
    slot_grad = spread(
        select,
        slot_prob.reshape(groups, local_experts * capacity, 1),
        full_grad.reshape(groups, parts, tok_rows, width),
        local_experts,
    )
    grad_acts = jnp.einsum("escd,ejd->escj", slot_grad, down_weight, preferred_element_type=F32)
    grad_hidden = grad_acts.astype(BF16)
    slot_sum = jnp.sum(grad_acts * hidden_acts.astype(F32), axis=3).swapaxes(0, 1)
    token_sum = jnp.sum(jnp.where(holds, slot_sum[..., None], 0.0), axis=2)
    route_sum = jnp.sum(jnp.where(named, token_sum[:, :, None, :], 0.0), axis=1)
    route_sum = lax.psum(lax.psum_scatter(route_sum, "ctx", scatter_dimension=0), "exp").T
    grad_logits = route_sum - route_probs * jnp.sum(route_sum, axis=1, keepdims=True)
    grad_weight = jnp.einsum(
        "escj,escd->ejd", hidden_acts, slot_grad, preferred_element_type=F32
    ).astype(BF16)
    return (combined, grad_logits, grad_hidden, grad_weight)


def solution(mesh):
    placed = (
        P("ctx", None, None, "exp"),
        P("ctx", "exp", None),
        P("ctx", None),
        P("ctx", None),
        P("ctx", "exp"),
    )
    return jax.shard_map(
        local,
        mesh=mesh,
        in_specs=placed,
        out_specs=(
            P("ctx", "exp"),
            P("ctx", None),
            P("ctx", None, None, "exp"),
            P("ctx", "exp", None),
        ),
        check_vma=False,
    )
```

```python
import functools

import jax
import jax.numpy as jnp
from jax import lax
from jax.experimental import pallas as pl
from jax.experimental.pallas import tpu as pltpu
from jax.sharding import PartitionSpec as P

MESH = pl.DeviceIdType.MESH
PAIR = 2
F32 = jnp.float32
BF16 = jnp.bfloat16


def exchange_kernel(
    outer,
    parts,
    acts_ref,
    weight_ref,
    prob_ref,
    back_ref,
    select_ref,
    grad_ref,
    full_ref,
    combined_ref,
    hidden_ref,
    slots_ref,
    dots_ref,
    weight_v,
    rows_v,
    away_v,
    home_v,
    core_v,
    far0_v,
    far1_v,
    near0_v,
    near1_v,
    last_v,
    load_sem,
    fetch_sem,
    az_s,
    az_r,
    au_s,
    au_r,
    av_s,
    av_r,
    ac_s,
    ac_r,
    rc_s,
    rc_r,
    rv_s,
    rv_r,
    ru_s,
    ru_r,
    rz_s,
    rz_r,
):
    ctx, y = lax.axis_index("ctx"), lax.axis_index("exp")
    z, x, c = ctx // (PAIR * PAIR), (ctx // PAIR) % PAIR, ctx % PAIR
    experts, capacity = rows_v.shape[1], rows_v.shape[2]
    tokens, width = grad_ref.shape
    half = tokens // 2
    spans = (pl.ds(0, half), pl.ds(half, half))

    def at_z(k):
        return (((z + k) % outer) * (PAIR * PAIR) + x * PAIR + c, y)

    def at_x(k):
        return (z * (PAIR * PAIR) + ((x + k) % PAIR) * PAIR + c, y)

    def at_y(k):
        return (ctx, (y + k) % parts)

    sibling = (z * (PAIR * PAIR) + x * PAIR + (1 - c), y)
    mid_to, mid_n = (at_x, at_y), (PAIR, parts)
    end_to, end_n = (at_y, at_x), (parts, PAIR)

    def send(src, dst, s, r, to):
        return pltpu.make_async_remote_copy(
            src_ref=src, dst_ref=dst, send_sem=s, recv_sem=r, device_id=to, device_id_type=MESH
        )

    loads = [
        pltpu.make_async_copy(weight_ref.at[e], weight_v.at[e], load_sem.at[e])
        for e in range(experts)
    ]
    for load in loads:
        load.start()
    own = pltpu.make_async_copy(grad_ref, full_ref.at[z, x, c, y], load_sem.at[experts])
    own.start()

    barrier = pltpu.get_barrier_semaphore()
    peers = [at_z(k) for k in range(1, outer)]
    peers += [at_x(k) for k in range(1, PAIR)]
    peers += [at_y(k) for k in range(1, parts)]
    peers += [sibling]
    for peer in peers:
        pl.semaphore_signal(barrier, inc=1, device_id=peer, device_id_type=MESH)
    pl.semaphore_wait(barrier, len(peers))

    def from_z(k):
        return (z - k + outer) % outer

    def gz(h, k):
        place = full_ref.at[z, x, c, y, spans[h]]
        return send(grad_ref.at[spans[h]], place, az_s.at[h, k], az_r.at[h, k], at_z(k))

    def gu(h, k, j):
        place = full_ref.at[from_z(k), x, c, y, spans[h]]
        return send(place, place, au_s.at[h, k, j], au_r.at[h, k, j], mid_to[h](j))

    def gv(h, k, j):
        if h == 0:
            place = full_ref.at[from_z(k), :, c, y, spans[h]]
        else:
            place = full_ref.at[from_z(k), x, c, :, spans[h]]
        return send(place, place, av_s.at[h, k, j], av_r.at[h, k, j], end_to[h](j))

    def gc(h, k):
        place = full_ref.at[from_z(k), :, c, :, spans[h]]
        return send(place, place, ac_s.at[h, k], ac_r.at[h, k], sibling)

    for k in range(1, outer):
        for h in range(2):
            gz(h, k).start()
    own.wait()

    def gather_mid(k):
        for h in range(2):
            if k:
                gz(h, k).wait_recv()
            for j in range(1, mid_n[h]):
                gu(h, k, j).start()

    def gather_end(k):
        for h in range(2):
            for j in range(1, mid_n[h]):
                gu(h, k, j).wait_recv()
            for j in range(1, end_n[h]):
                gv(h, k, j).start()

    def gather_core(k):
        for h in range(2):
            for j in range(1, end_n[h]):
                gv(h, k, j).wait_recv()
            gc(h, k).start()

    gather_mid(0)

    block = acts_ref.shape[1] // 2
    groups = block // capacity

    def product(e, m):
        start = pl.multiple_of(m * block, block)
        value = lax.dot_general(
            acts_ref[e, pl.ds(start, block), :],
            weight_v[e],
            (((1,), (1,)), ((), ())),
            preferred_element_type=F32,
        )
        prob = prob_ref[pl.ds(m * groups, groups), e].reshape(block, 1)
        value = (value * prob).astype(BF16)
        rows_v[pl.ds(m * groups, groups), e] = value.reshape(groups, capacity, value.shape[1])

    for e in range(experts):
        loads[e].wait()
        if e == 0:
            gather_end(0)
        else:
            for k in range(1, outer):
                gather_mid(k)
        lax.fori_loop(0, 2, lambda m, _: (product(e, m), 0)[1], 0)

    for k in range(1, outer):
        gather_end(k)

    order = list(range(1, outer)) + [0]

    def rc(i):
        zi = (z + order[i]) % outer
        return send(away_v.at[i % 2], core_v.at[zi], rc_s.at[i], rc_r.at[i], sibling)

    def rv(h, i, j):
        zi = (z + order[i]) % outer
        if h == 0:
            src, dst = home_v.at[zi, :, (y + j) % parts, spans[0]], far0_v.at[zi, j - 1]
        else:
            src, dst = home_v.at[zi, (x + j) % PAIR, :, spans[1]], far1_v.at[zi, j - 1]
        return send(src, dst, rv_s.at[h, i, j], rv_r.at[h, i, j], end_to[h](j))

    def ru(h, i, j):
        zi = (z + order[i]) % outer
        if h == 0:
            src, dst = far0_v.at[zi, 0, (x + j) % PAIR], near0_v.at[zi, j - 1]
        else:
            src, dst = far1_v.at[zi, 0, (y + j) % parts], near1_v.at[zi, j - 1]
        return send(src, dst, ru_s.at[h, i, j], ru_r.at[h, i, j], mid_to[h](j))

    near = (near0_v, near1_v)

    def rz(h, k):
        zi = (z + k) % outer
        return send(near[h].at[zi, 0], last_v.at[h, k - 1], rz_s.at[h, k], rz_r.at[h, k], at_z(k))

    def mix(zi, xi, ci, put):
        group = zi * (PAIR * PAIR) + xi * PAIR + ci
        value = jnp.dot(
            back_ref[group],
            rows_v[group].reshape(experts * capacity, rows_v.shape[3]),
            preferred_element_type=F32,
        ).astype(BF16)
        for part in range(parts):
            put(xi, part, value[:, part * width : (part + 1) * width])

    for i in range(outer):
        zi = (z + order[i]) % outer
        if i >= 2:
            rc(i - 2).wait_send()

        def put_away(xi, part, value):
            away_v[i % 2, xi, part] = value

        def put_home(xi, part, value):
            home_v[zi, xi, part] = value

        lax.fori_loop(0, PAIR, lambda xi, _: (mix(zi, xi, 1 - c, put_away), 0)[1], 0)
        rc(i).start()
        lax.fori_loop(0, PAIR, lambda xi, _: (mix(zi, xi, c, put_home), 0)[1], 0)
        gather_core(i)

    def add(first, others):
        total = first.astype(F32)
        for other in others:
            total = total + other.astype(F32)
        return total.astype(BF16)

    def sum_core(i):
        zi = (z + order[i]) % outer
        rc(i).wait_recv()

        def step(n, _):
            xi, part = n // parts, n % parts
            home_v[zi, xi, part] = add(home_v[zi, xi, part], [core_v[zi, xi, part]])
            return 0

        lax.fori_loop(0, PAIR * parts, step, 0)
        for h in range(2):
            for j in range(1, end_n[h]):
                rv(h, i, j).start()

    def sum_end(i):
        zi = (z + order[i]) % outer
        for h in range(2):
            for j in range(1, end_n[h]):
                rv(h, i, j).wait_recv()
        for xi in range(PAIR):
            others = [far0_v[zi, j - 1, xi] for j in range(1, end_n[0])]
            far0_v[zi, 0, xi] = add(home_v[zi, xi, y, spans[0]], others)
        for part in range(parts):
            others = [far1_v[zi, j - 1, part] for j in range(1, end_n[1])]
            far1_v[zi, 0, part] = add(home_v[zi, x, part, spans[1]], others)
        for h in range(2):
            for j in range(1, mid_n[h]):
                ru(h, i, j).start()

    def sum_mid(i):
        zi = (z + order[i]) % outer
        for h in range(2):
            for j in range(1, mid_n[h]):
                ru(h, i, j).wait_recv()
            others = [near[h][zi, j - 1] for j in range(1, mid_n[h])]
            mine = far0_v[zi, 0, x] if h == 0 else far1_v[zi, 0, y]
            near[h][zi, 0] = add(mine, others)
            if order[i]:
                rz(h, order[i]).start()

    for i in range(outer):
        sum_core(i)
    for h in range(2):
        for k in range(outer):
            gc(h, k).wait_recv()

    def fetch(i, ci):
        zi = (z + order[i]) % outer
        return pltpu.make_async_copy(full_ref.at[zi, :, ci], core_v.at[zi], fetch_sem.at[i, ci])

    def spread(i, ci):
        zi = (z + order[i]) % outer
        fetch(i, ci).wait()

        def step(xi, _):
            group = zi * (PAIR * PAIR) + xi * PAIR + ci
            prob = prob_ref[group].reshape(experts * capacity, 1)
            for part in range(parts):
                value = jnp.dot(
                    select_ref[group], core_v[zi, xi, part], preferred_element_type=F32
                )
                rows_v[group, :, :, part * width : (part + 1) * width] = (
                    (value * prob).astype(BF16).reshape(experts, capacity, width)
                )
            return 0

        lax.fori_loop(0, PAIR, step, 0)

    for i in range(outer):
        fetch(i, 0).start()
    for i in range(outer):
        spread(i, 0)
        fetch(i, 1).start()
        sum_end(i)
        if i:
            sum_mid(i - 1)
    for i in range(outer):
        spread(i, 1)
    stores = [
        pltpu.make_async_copy(rows_v.at[:, e], slots_ref.at[e], load_sem.at[e])
        for e in range(experts)
    ]
    for store in stores:
        store.start()

    def pull(n, _):
        e, m = n // 2, n % 2
        start = pl.multiple_of(m * block, block)
        value = jnp.dot(
            rows_v[pl.ds(m * groups, groups), e].reshape(block, rows_v.shape[3]),
            weight_v[e],
            preferred_element_type=F32,
        )
        hidden_ref[e, pl.ds(start, block), :] = value.astype(BF16)
        dots_ref[e, pl.ds(start, block), :] = jnp.sum(
            value * acts_ref[e, pl.ds(start, block), :].astype(F32), axis=1, keepdims=True
        )
        return 0

    lax.fori_loop(0, 2 * experts, pull, 0)
    sum_mid(outer - 1)

    for h in range(2):
        for k in range(1, outer):
            rz(h, k).wait_recv()
        combined_ref[spans[h], :] = add(
            near[h][z, 0], [last_v[h, k - 1] for k in range(1, outer)]
        )

    for h in range(2):
        for k in range(outer):
            if k:
                gz(h, k).wait_send()
                rz(h, k).wait_send()
            for j in range(1, mid_n[h]):
                gu(h, k, j).wait_send()
                ru(h, k, j).wait_send()
            for j in range(1, end_n[h]):
                gv(h, k, j).wait_send()
                rv(h, k, j).wait_send()
            gc(h, k).wait_send()
    for i in range(max(0, outer - 2), outer):
        rc(i).wait_send()
    for store in stores:
        store.wait()


def exchange(acts, weight, slot_prob, back, select, out_grad, outer, parts):
    experts, slots, _ = acts.shape
    groups = outer * PAIR * PAIR
    capacity = slots // groups
    tokens, width = out_grad.shape
    full = parts * width
    half = tokens // 2
    vmem = pl.BlockSpec(memory_space=pltpu.VMEM)
    hbm = pl.BlockSpec(memory_space=pl.ANY)
    dma = pltpu.SemaphoreType.DMA
    most = max(PAIR, parts)
    pairs = [(2, outer), (2, outer, most), (2, outer, most), (2, outer)]
    pairs += [(outer,), (2, outer, most), (2, outer, most), (2, outer)]
    sems = [dma((experts + 1,)), dma((outer, 2))]
    for shape in pairs:
        sems += [dma(shape), dma(shape)]
    return pl.pallas_call(
        functools.partial(exchange_kernel, outer, parts),
        out_shape=(
            jax.ShapeDtypeStruct((outer, PAIR, PAIR, parts, tokens, width), BF16),
            jax.ShapeDtypeStruct((tokens, width), BF16),
            jax.ShapeDtypeStruct(acts.shape, BF16),
            jax.ShapeDtypeStruct((experts, groups, capacity, full), BF16),
            jax.ShapeDtypeStruct((experts, slots, 1), F32),
        ),
        in_specs=[vmem, hbm, vmem, vmem, vmem, hbm],
        out_specs=(hbm, vmem, vmem, hbm, vmem),
        scratch_shapes=[
            pltpu.VMEM(weight.shape, BF16),
            pltpu.VMEM((groups, experts, capacity, full), BF16),
            pltpu.VMEM((2, PAIR, parts, tokens, width), BF16),
            pltpu.VMEM((outer, PAIR, parts, tokens, width), BF16),
            pltpu.VMEM((outer, PAIR, parts, tokens, width), BF16),
            pltpu.VMEM((outer, parts - 1, PAIR, half, width), BF16),
            pltpu.VMEM((outer, PAIR - 1, parts, half, width), BF16),
            pltpu.VMEM((outer, PAIR - 1, half, width), BF16),
            pltpu.VMEM((outer, parts - 1, half, width), BF16),
            pltpu.VMEM((2, outer - 1, half, width), BF16),
        ]
        + sems,
        compiler_params=pltpu.CompilerParams(
            collective_id=0, has_side_effects=True, vmem_limit_bytes=62 * 1024 * 1024
        ),
        cost_estimate=pl.CostEstimate(
            flops=4 * experts * slots * weight.shape[2] * full,
            bytes_accessed=4 * weight.size,
            transcendentals=0,
        ),
    )(acts, weight, slot_prob, back, select, out_grad)


def routes_kernel(outer, mine_ref, all_ref, z_s, z_r, x_s, x_r, c_s, c_r):
    ctx, y = lax.axis_index("ctx"), lax.axis_index("exp")
    z, x, c = ctx // (PAIR * PAIR), (ctx // PAIR) % PAIR, ctx % PAIR
    to_z = [(((z + k) % outer) * (PAIR * PAIR) + x * PAIR + c, y) for k in range(1, outer)]
    to_x = (z * (PAIR * PAIR) + (1 - x) * PAIR + c, y)
    to_c = (z * (PAIR * PAIR) + x * PAIR + (1 - c), y)
    barrier = pltpu.get_barrier_semaphore()
    for peer in to_z + [to_x, to_c]:
        pl.semaphore_signal(barrier, inc=1, device_id=peer, device_id_type=MESH)
    pl.semaphore_wait(barrier, outer + 1)

    def send(src, dst, s, r, to):
        copy = pltpu.make_async_remote_copy(
            src_ref=src, dst_ref=dst, send_sem=s, recv_sem=r, device_id=to, device_id_type=MESH
        )
        copy.start()
        return copy

    place = all_ref.at[z, x, c]
    along = [
        send(mine_ref, place, z_s.at[k], z_r.at[k], peer) for k, peer in enumerate(to_z)
    ]
    all_ref[z, x, c] = mine_ref[...]
    for copy in along:
        copy.wait()
    place = all_ref.at[:, x, c]
    send(place, place, x_s, x_r, to_x).wait()
    place = all_ref.at[:, :, c]
    send(place, place, c_s, c_r, to_c).wait()


def gather_routes(mine, outer):
    vmem = pl.BlockSpec(memory_space=pltpu.VMEM)
    dma = pltpu.SemaphoreType.DMA
    return pl.pallas_call(
        functools.partial(routes_kernel, outer),
        out_shape=jax.ShapeDtypeStruct((outer, PAIR, PAIR) + mine.shape, mine.dtype),
        in_specs=[vmem],
        out_specs=vmem,
        scratch_shapes=[dma((outer,)), dma((outer,)), dma, dma, dma, dma],
        compiler_params=pltpu.CompilerParams(collective_id=1, has_side_effects=True),
    )(mine)


def total_kernel(
    outer, parts, all_ref, out_ref, c_v, x_v, z_v, y_v, sum_c, sum_x,
    c_s, c_r, x_s, x_r, z_s, z_r, y_s, y_r,
):
    ctx, y = lax.axis_index("ctx"), lax.axis_index("exp")
    z, x, c = ctx // (PAIR * PAIR), (ctx // PAIR) % PAIR, ctx % PAIR
    to_z = [(((z + k) % outer) * (PAIR * PAIR) + x * PAIR + c, y) for k in range(1, outer)]
    to_y = [(ctx, (y + k) % parts) for k in range(1, parts)]
    to_x = (z * (PAIR * PAIR) + (1 - x) * PAIR + c, y)
    to_c = (z * (PAIR * PAIR) + x * PAIR + (1 - c), y)
    barrier = pltpu.get_barrier_semaphore()
    for peer in to_z + to_y + [to_x, to_c]:
        pl.semaphore_signal(barrier, inc=1, device_id=peer, device_id_type=MESH)
    pl.semaphore_wait(barrier, outer + parts)

    def send(src, dst, s, r, to):
        copy = pltpu.make_async_remote_copy(
            src_ref=src, dst_ref=dst, send_sem=s, recv_sem=r, device_id=to, device_id_type=MESH
        )
        copy.start()
        return copy

    send(all_ref.at[:, :, 1 - c], c_v, c_s, c_r, to_c).wait()
    sum_c[...] = all_ref[:, :, c] + c_v[...]
    send(sum_c.at[:, 1 - x], x_v, x_s, x_r, to_x).wait()
    sum_x[...] = sum_c[:, x] + x_v[...]
    along = [
        send(sum_x.at[(z + k) % outer], z_v.at[k - 1], z_s.at[k], z_r.at[k], to_z[k - 1])
        for k in range(1, outer)
    ]
    for copy in along:
        copy.wait()
    total = sum_x[z]
    for k in range(1, outer):
        total = total + z_v[k - 1]
    y_v[y] = total
    place = y_v.at[y]
    along = [send(place, place, y_s.at[k], y_r.at[k], to_y[k - 1]) for k in range(1, parts)]
    for copy in along:
        copy.wait()
    out_ref[...] = jnp.sum(y_v[...], axis=0)


def total_routes(values, outer, parts):
    one = values.shape[3:]
    vmem = pl.BlockSpec(memory_space=pltpu.VMEM)
    dma = pltpu.SemaphoreType.DMA
    return pl.pallas_call(
        functools.partial(total_kernel, outer, parts),
        out_shape=jax.ShapeDtypeStruct(one, F32),
        in_specs=[vmem],
        out_specs=vmem,
        scratch_shapes=[
            pltpu.VMEM((outer, PAIR) + one, F32),
            pltpu.VMEM((outer,) + one, F32),
            pltpu.VMEM((outer - 1,) + one, F32),
            pltpu.VMEM((parts,) + one, F32),
            pltpu.VMEM((outer, PAIR) + one, F32),
            pltpu.VMEM((outer,) + one, F32),
            dma, dma, dma, dma, dma((outer,)), dma((outer,)), dma((parts,)), dma((parts,)),
        ],
        compiler_params=pltpu.CompilerParams(collective_id=2, has_side_effects=True),
    )(values)


def local(hidden_acts, down_weight, expert_ids, route_logits, out_grad):
    local_experts, groups, capacity, hidden = hidden_acts.shape
    tok_rows, top_count = expert_ids.shape
    width = out_grad.shape[1]
    parts = lax.axis_size("exp")
    first = lax.axis_index("ctx") * local_experts

    weights = jnp.exp(route_logits)
    route_probs = weights / jnp.sum(weights, axis=1, keepdims=True)

    outer = groups // (PAIR * PAIR)
    routes = gather_routes(
        jnp.concatenate([expert_ids.astype(F32), route_probs], axis=1).T, outer
    ).reshape(groups, 2 * top_count, tok_rows)
    ids = routes[:, :top_count].astype(jnp.int32)
    probs = routes[:, top_count:]

    mine = first + jnp.arange(local_experts, dtype=jnp.int32)
    named = ids[:, None] == mine[None, :, None, None]
    taken = jnp.any(named, axis=2)
    prob_of = jnp.sum(jnp.where(named, probs[:, None], 0.0), axis=2)
    order = jnp.arange(tok_rows)
    earlier = (order[:, None] < order[None, :]).astype(BF16)
    position = jnp.einsum(
        "cet,tu->ceu", taken.astype(BF16), earlier, preferred_element_type=F32
    ).astype(jnp.int32)
    slots = jnp.arange(capacity, dtype=jnp.int32)
    holds = taken[:, :, None, :] & (position[:, :, None, :] == slots[:, None])
    slot_prob = jnp.sum(jnp.where(holds, prob_of[:, :, None, :], 0.0), axis=3)
    select = holds.astype(BF16).reshape(groups, local_experts * capacity, tok_rows)
    back = select.swapaxes(1, 2)

    _, combined, grad_hidden, slot_grad, slot_sum = exchange(
        hidden_acts.reshape(local_experts, groups * capacity, hidden),
        down_weight.swapaxes(1, 2),
        slot_prob[..., None],
        back,
        select,
        out_grad,
        outer,
        parts,
    )
    grad_hidden = grad_hidden.reshape(hidden_acts.shape)
    slot_sum = slot_sum.reshape(local_experts, groups, capacity).swapaxes(0, 1)
    token_sum = jnp.sum(jnp.where(holds, slot_sum[..., None], 0.0), axis=2)
    route_sum = jnp.sum(jnp.where(named, token_sum[:, :, None, :], 0.0), axis=1)
    route_sum = jnp.pad(route_sum, ((0, 0), (0, top_count), (0, 0)))
    route_sum = total_routes(
        route_sum.reshape(outer, PAIR, PAIR, 2 * top_count, tok_rows), outer, parts
    )[:top_count].T
    grad_logits = route_sum - route_probs * jnp.sum(route_sum, axis=1, keepdims=True)
    grad_weight = jnp.einsum(
        "escj,escd->ejd", hidden_acts, slot_grad, preferred_element_type=F32
    ).astype(BF16)
    return (combined, grad_logits, grad_hidden, grad_weight)


def solution(mesh):
    placed = (
        P("ctx", None, None, "exp"),
        P("ctx", "exp", None),
        P("ctx", None),
        P("ctx", None),
        P("ctx", "exp"),
    )
    return jax.shard_map(
        local,
        mesh=mesh,
        in_specs=placed,
        out_specs=(
            P("ctx", "exp"),
            P("ctx", None),
            P("ctx", None, None, "exp"),
            P("ctx", "exp", None),
        ),
        check_vma=False,
    )
```

```python
import functools

import jax
import jax.numpy as jnp
from jax import lax
from jax.experimental import pallas as pl
from jax.experimental.pallas import tpu as pltpu
from jax.sharding import PartitionSpec as P

MESH = pl.DeviceIdType.MESH
PAIR = 2
F32 = jnp.float32
BF16 = jnp.bfloat16


def exchange_kernel(
    outer,
    parts,
    acts_ref,
    weight_ref,
    prob_ref,
    back_ref,
    select_ref,
    grad_ref,
    full_ref,
    combined_ref,
    hidden_ref,
    slots_ref,
    dots_ref,
    weight_v,
    rows_v,
    away_v,
    home_v,
    core_v,
    far0_v,
    far1_v,
    near0_v,
    near1_v,
    last_v,
    load_sem,
    fetch_sem,
    az_s,
    az_r,
    au_s,
    au_r,
    av_s,
    av_r,
    ac_s,
    ac_r,
    rc_s,
    rc_r,
    rv_s,
    rv_r,
    ru_s,
    ru_r,
    rz_s,
    rz_r,
):
    ctx, y = lax.axis_index("ctx"), lax.axis_index("exp")
    z, x, c = ctx // (PAIR * PAIR), (ctx // PAIR) % PAIR, ctx % PAIR
    experts, capacity = rows_v.shape[1], rows_v.shape[2]
    tokens, width = grad_ref.shape
    half = tokens // 2
    spans = (pl.ds(0, half), pl.ds(half, half))

    def at_z(k):
        return (((z + k) % outer) * (PAIR * PAIR) + x * PAIR + c, y)

    def at_x(k):
        return (z * (PAIR * PAIR) + ((x + k) % PAIR) * PAIR + c, y)

    def at_y(k):
        return (ctx, (y + k) % parts)

    sibling = (z * (PAIR * PAIR) + x * PAIR + (1 - c), y)
    mid_to, mid_n = (at_x, at_y), (PAIR, parts)
    end_to, end_n = (at_y, at_x), (parts, PAIR)

    def send(src, dst, s, r, to):
        return pltpu.make_async_remote_copy(
            src_ref=src, dst_ref=dst, send_sem=s, recv_sem=r, device_id=to, device_id_type=MESH
        )

    loads = [
        pltpu.make_async_copy(weight_ref.at[e], weight_v.at[e], load_sem.at[e])
        for e in range(experts)
    ]
    for load in loads:
        load.start()
    own = pltpu.make_async_copy(grad_ref, full_ref.at[z, x, c, y], load_sem.at[experts])
    own.start()

    barrier = pltpu.get_barrier_semaphore()
    peers = [at_z(k) for k in range(1, outer)]
    peers += [at_x(k) for k in range(1, PAIR)]
    peers += [at_y(k) for k in range(1, parts)]
    peers += [sibling]
    for peer in peers:
        pl.semaphore_signal(barrier, inc=1, device_id=peer, device_id_type=MESH)
    pl.semaphore_wait(barrier, len(peers))

    def from_z(k):
        return (z - k + outer) % outer

    def gz(h, k):
        place = full_ref.at[z, x, c, y, spans[h]]
        return send(grad_ref.at[spans[h]], place, az_s.at[h, k], az_r.at[h, k], at_z(k))

    def gu(h, k, j):
        place = full_ref.at[from_z(k), x, c, y, spans[h]]
        return send(place, place, au_s.at[h, k, j], au_r.at[h, k, j], mid_to[h](j))

    def gv(h, k, j):
        if h == 0:
            place = full_ref.at[from_z(k), :, c, y, spans[h]]
        else:
            place = full_ref.at[from_z(k), x, c, :, spans[h]]
        return send(place, place, av_s.at[h, k, j], av_r.at[h, k, j], end_to[h](j))

    def gc(h, k):
        place = full_ref.at[from_z(k), :, c, :, spans[h]]
        return send(place, place, ac_s.at[h, k], ac_r.at[h, k], sibling)

    for k in range(1, outer):
        for h in range(2):
            gz(h, k).start()
    own.wait()

    def gather_mid(k):
        for h in range(2):
            if k:
                gz(h, k).wait_recv()
            for j in range(1, mid_n[h]):
                gu(h, k, j).start()

    def gather_end(k):
        for h in range(2):
            for j in range(1, mid_n[h]):
                gu(h, k, j).wait_recv()
            for j in range(1, end_n[h]):
                gv(h, k, j).start()

    def gather_core(k):
        for h in range(2):
            for j in range(1, end_n[h]):
                gv(h, k, j).wait_recv()
            gc(h, k).start()

    gather_mid(0)

    block = acts_ref.shape[1] // 2
    groups = block // capacity

    def product(e, m):
        start = pl.multiple_of(m * block, block)
        value = lax.dot_general(
            acts_ref[e, pl.ds(start, block), :],
            weight_v[e],
            (((1,), (1,)), ((), ())),
            preferred_element_type=F32,
        )
        prob = prob_ref[pl.ds(m * groups, groups), e].reshape(block, 1)
        value = (value * prob).astype(BF16)
        rows_v[pl.ds(m * groups, groups), e] = value.reshape(groups, capacity, value.shape[1])

    for e in range(experts):
        loads[e].wait()
        if e == 0:
            gather_end(0)
        else:
            for k in range(1, outer):
                gather_mid(k)
        lax.fori_loop(0, 2, lambda m, _: (product(e, m), 0)[1], 0)

    for k in range(1, outer):
        gather_end(k)

    order = list(range(1, outer)) + [0]

    def rc(i):
        zi = (z + order[i]) % outer
        return send(away_v.at[i % 2], core_v.at[zi], rc_s.at[i], rc_r.at[i], sibling)

    def rv(h, i, j):
        zi = (z + order[i]) % outer
        if h == 0:
            src, dst = home_v.at[zi, :, (y + j) % parts, spans[0]], far0_v.at[zi, j - 1]
        else:
            src, dst = home_v.at[zi, (x + j) % PAIR, :, spans[1]], far1_v.at[zi, j - 1]
        return send(src, dst, rv_s.at[h, i, j], rv_r.at[h, i, j], end_to[h](j))

    def ru(h, i, j):
        zi = (z + order[i]) % outer
        if h == 0:
            src, dst = far0_v.at[zi, 0, (x + j) % PAIR], near0_v.at[zi, j - 1]
        else:
            src, dst = far1_v.at[zi, 0, (y + j) % parts], near1_v.at[zi, j - 1]
        return send(src, dst, ru_s.at[h, i, j], ru_r.at[h, i, j], mid_to[h](j))

    near = (near0_v, near1_v)

    def rz(h, k):
        zi = (z + k) % outer
        return send(near[h].at[zi, 0], last_v.at[h, k - 1], rz_s.at[h, k], rz_r.at[h, k], at_z(k))

    def mix(zi, xi, ci, put):
        group = zi * (PAIR * PAIR) + xi * PAIR + ci
        value = jnp.dot(
            back_ref[group],
            rows_v[group].reshape(experts * capacity, rows_v.shape[3]),
            preferred_element_type=F32,
        ).astype(BF16)
        for part in range(parts):
            put(xi, part, value[:, part * width : (part + 1) * width])

    for i in range(outer):
        zi = (z + order[i]) % outer
        if i >= 2:
            rc(i - 2).wait_send()

        def put_away(xi, part, value):
            away_v[i % 2, xi, part] = value

        def put_home(xi, part, value):
            home_v[zi, xi, part] = value

        lax.fori_loop(0, PAIR, lambda xi, _: (mix(zi, xi, 1 - c, put_away), 0)[1], 0)
        rc(i).start()
        lax.fori_loop(0, PAIR, lambda xi, _: (mix(zi, xi, c, put_home), 0)[1], 0)

    def add(first, others):
        total = first.astype(F32)
        for other in others:
            total = total + other.astype(F32)
        return total.astype(BF16)

    def sum_core(i):
        zi = (z + order[i]) % outer
        rc(i).wait_recv()

        def step(n, _):
            xi, part = n // parts, n % parts
            home_v[zi, xi, part] = add(home_v[zi, xi, part], [core_v[zi, xi, part]])
            return 0

        lax.fori_loop(0, PAIR * parts, step, 0)
        for h in range(2):
            for j in range(1, end_n[h]):
                rv(h, i, j).start()

    def sum_end(i):
        zi = (z + order[i]) % outer
        for h in range(2):
            for j in range(1, end_n[h]):
                rv(h, i, j).wait_recv()
        for xi in range(PAIR):
            others = [far0_v[zi, j - 1, xi] for j in range(1, end_n[0])]
            far0_v[zi, 0, xi] = add(home_v[zi, xi, y, spans[0]], others)
        for part in range(parts):
            others = [far1_v[zi, j - 1, part] for j in range(1, end_n[1])]
            far1_v[zi, 0, part] = add(home_v[zi, x, part, spans[1]], others)
        for h in range(2):
            for j in range(1, mid_n[h]):
                ru(h, i, j).start()

    def sum_mid(i):
        zi = (z + order[i]) % outer
        for h in range(2):
            for j in range(1, mid_n[h]):
                ru(h, i, j).wait_recv()
            others = [near[h][zi, j - 1] for j in range(1, mid_n[h])]
            mine = far0_v[zi, 0, x] if h == 0 else far1_v[zi, 0, y]
            near[h][zi, 0] = add(mine, others)
            if order[i]:
                rz(h, order[i]).start()

    for i in range(outer):
        sum_core(i)
    for k in range(outer):
        gather_core(k)
    for h in range(2):
        for k in range(outer):
            gc(h, k).wait_recv()

    def fetch(i, ci):
        zi = (z + order[i]) % outer
        return pltpu.make_async_copy(full_ref.at[zi, :, ci], core_v.at[zi], fetch_sem.at[i, ci])

    def spread(i, ci):
        zi = (z + order[i]) % outer
        fetch(i, ci).wait()

        def step(xi, _):
            group = zi * (PAIR * PAIR) + xi * PAIR + ci
            prob = prob_ref[group].reshape(experts * capacity, 1)
            for part in range(parts):
                value = jnp.dot(
                    select_ref[group], core_v[zi, xi, part], preferred_element_type=F32
                )
                rows_v[group, :, :, part * width : (part + 1) * width] = (
                    (value * prob).astype(BF16).reshape(experts, capacity, width)
                )
            return 0

        lax.fori_loop(0, PAIR, step, 0)

    for i in range(outer):
        fetch(i, 0).start()
    for i in range(outer):
        spread(i, 0)
        fetch(i, 1).start()
        sum_end(i)
        if i:
            sum_mid(i - 1)
    for i in range(outer):
        spread(i, 1)
    stores = [
        pltpu.make_async_copy(rows_v.at[:, e], slots_ref.at[e], load_sem.at[e])
        for e in range(experts)
    ]
    for store in stores:
        store.start()

    def pull(n, _):
        e, m = n // 2, n % 2
        start = pl.multiple_of(m * block, block)
        value = jnp.dot(
            rows_v[pl.ds(m * groups, groups), e].reshape(block, rows_v.shape[3]),
            weight_v[e],
            preferred_element_type=F32,
        )
        hidden_ref[e, pl.ds(start, block), :] = value.astype(BF16)
        dots_ref[e, pl.ds(start, block), :] = jnp.sum(
            value * acts_ref[e, pl.ds(start, block), :].astype(F32), axis=1, keepdims=True
        )
        return 0

    lax.fori_loop(0, 2 * experts, pull, 0)
    sum_mid(outer - 1)

    for h in range(2):
        for k in range(1, outer):
            rz(h, k).wait_recv()
        combined_ref[spans[h], :] = add(
            near[h][z, 0], [last_v[h, k - 1] for k in range(1, outer)]
        )

    for h in range(2):
        for k in range(outer):
            if k:
                gz(h, k).wait_send()
                rz(h, k).wait_send()
            for j in range(1, mid_n[h]):
                gu(h, k, j).wait_send()
                ru(h, k, j).wait_send()
            for j in range(1, end_n[h]):
                gv(h, k, j).wait_send()
                rv(h, k, j).wait_send()
            gc(h, k).wait_send()
    for i in range(max(0, outer - 2), outer):
        rc(i).wait_send()
    for store in stores:
        store.wait()


def exchange(acts, weight, slot_prob, back, select, out_grad, outer, parts):
    experts, slots, _ = acts.shape
    groups = outer * PAIR * PAIR
    capacity = slots // groups
    tokens, width = out_grad.shape
    full = parts * width
    half = tokens // 2
    vmem = pl.BlockSpec(memory_space=pltpu.VMEM)
    hbm = pl.BlockSpec(memory_space=pl.ANY)
    dma = pltpu.SemaphoreType.DMA
    most = max(PAIR, parts)
    pairs = [(2, outer), (2, outer, most), (2, outer, most), (2, outer)]
    pairs += [(outer,), (2, outer, most), (2, outer, most), (2, outer)]
    sems = [dma((experts + 1,)), dma((outer, 2))]
    for shape in pairs:
        sems += [dma(shape), dma(shape)]
    return pl.pallas_call(
        functools.partial(exchange_kernel, outer, parts),
        out_shape=(
            jax.ShapeDtypeStruct((outer, PAIR, PAIR, parts, tokens, width), BF16),
            jax.ShapeDtypeStruct((tokens, width), BF16),
            jax.ShapeDtypeStruct(acts.shape, BF16),
            jax.ShapeDtypeStruct((experts, groups, capacity, full), BF16),
            jax.ShapeDtypeStruct((experts, slots, 1), F32),
        ),
        in_specs=[vmem, hbm, vmem, vmem, vmem, hbm],
        out_specs=(hbm, vmem, vmem, hbm, vmem),
        scratch_shapes=[
            pltpu.VMEM(weight.shape, BF16),
            pltpu.VMEM((groups, experts, capacity, full), BF16),
            pltpu.VMEM((2, PAIR, parts, tokens, width), BF16),
            pltpu.VMEM((outer, PAIR, parts, tokens, width), BF16),
            pltpu.VMEM((outer, PAIR, parts, tokens, width), BF16),
            pltpu.VMEM((outer, parts - 1, PAIR, half, width), BF16),
            pltpu.VMEM((outer, PAIR - 1, parts, half, width), BF16),
            pltpu.VMEM((outer, PAIR - 1, half, width), BF16),
            pltpu.VMEM((outer, parts - 1, half, width), BF16),
            pltpu.VMEM((2, outer - 1, half, width), BF16),
        ]
        + sems,
        compiler_params=pltpu.CompilerParams(
            collective_id=0, has_side_effects=True, vmem_limit_bytes=62 * 1024 * 1024
        ),
        cost_estimate=pl.CostEstimate(
            flops=4 * experts * slots * weight.shape[2] * full,
            bytes_accessed=4 * weight.size,
            transcendentals=0,
        ),
    )(acts, weight, slot_prob, back, select, out_grad)


def routes_kernel(outer, mine_ref, all_ref, z_s, z_r, x_s, x_r, c_s, c_r):
    ctx, y = lax.axis_index("ctx"), lax.axis_index("exp")
    z, x, c = ctx // (PAIR * PAIR), (ctx // PAIR) % PAIR, ctx % PAIR
    to_z = [(((z + k) % outer) * (PAIR * PAIR) + x * PAIR + c, y) for k in range(1, outer)]
    to_x = (z * (PAIR * PAIR) + (1 - x) * PAIR + c, y)
    to_c = (z * (PAIR * PAIR) + x * PAIR + (1 - c), y)
    barrier = pltpu.get_barrier_semaphore()
    for peer in to_z + [to_x, to_c]:
        pl.semaphore_signal(barrier, inc=1, device_id=peer, device_id_type=MESH)
    pl.semaphore_wait(barrier, outer + 1)

    def send(src, dst, s, r, to):
        copy = pltpu.make_async_remote_copy(
            src_ref=src, dst_ref=dst, send_sem=s, recv_sem=r, device_id=to, device_id_type=MESH
        )
        copy.start()
        return copy

    place = all_ref.at[z, x, c]
    along = [
        send(mine_ref, place, z_s.at[k], z_r.at[k], peer) for k, peer in enumerate(to_z)
    ]
    all_ref[z, x, c] = mine_ref[...]
    for copy in along:
        copy.wait()
    place = all_ref.at[:, x, c]
    send(place, place, x_s, x_r, to_x).wait()
    place = all_ref.at[:, :, c]
    send(place, place, c_s, c_r, to_c).wait()


def gather_routes(mine, outer):
    vmem = pl.BlockSpec(memory_space=pltpu.VMEM)
    dma = pltpu.SemaphoreType.DMA
    return pl.pallas_call(
        functools.partial(routes_kernel, outer),
        out_shape=jax.ShapeDtypeStruct((outer, PAIR, PAIR) + mine.shape, mine.dtype),
        in_specs=[vmem],
        out_specs=vmem,
        scratch_shapes=[dma((outer,)), dma((outer,)), dma, dma, dma, dma],
        compiler_params=pltpu.CompilerParams(collective_id=1, has_side_effects=True),
    )(mine)


def total_kernel(
    outer, parts, all_ref, out_ref, c_v, x_v, z_v, y_v, sum_c, sum_x,
    c_s, c_r, x_s, x_r, z_s, z_r, y_s, y_r,
):
    ctx, y = lax.axis_index("ctx"), lax.axis_index("exp")
    z, x, c = ctx // (PAIR * PAIR), (ctx // PAIR) % PAIR, ctx % PAIR
    to_z = [(((z + k) % outer) * (PAIR * PAIR) + x * PAIR + c, y) for k in range(1, outer)]
    to_y = [(ctx, (y + k) % parts) for k in range(1, parts)]
    to_x = (z * (PAIR * PAIR) + (1 - x) * PAIR + c, y)
    to_c = (z * (PAIR * PAIR) + x * PAIR + (1 - c), y)
    barrier = pltpu.get_barrier_semaphore()
    for peer in to_z + to_y + [to_x, to_c]:
        pl.semaphore_signal(barrier, inc=1, device_id=peer, device_id_type=MESH)
    pl.semaphore_wait(barrier, outer + parts)

    def send(src, dst, s, r, to):
        copy = pltpu.make_async_remote_copy(
            src_ref=src, dst_ref=dst, send_sem=s, recv_sem=r, device_id=to, device_id_type=MESH
        )
        copy.start()
        return copy

    send(all_ref.at[:, :, 1 - c], c_v, c_s, c_r, to_c).wait()
    sum_c[...] = all_ref[:, :, c] + c_v[...]
    send(sum_c.at[:, 1 - x], x_v, x_s, x_r, to_x).wait()
    sum_x[...] = sum_c[:, x] + x_v[...]
    along = [
        send(sum_x.at[(z + k) % outer], z_v.at[k - 1], z_s.at[k], z_r.at[k], to_z[k - 1])
        for k in range(1, outer)
    ]
    for copy in along:
        copy.wait()
    total = sum_x[z]
    for k in range(1, outer):
        total = total + z_v[k - 1]
    y_v[y] = total
    place = y_v.at[y]
    along = [send(place, place, y_s.at[k], y_r.at[k], to_y[k - 1]) for k in range(1, parts)]
    for copy in along:
        copy.wait()
    out_ref[...] = jnp.sum(y_v[...], axis=0)


def total_routes(values, outer, parts):
    one = values.shape[3:]
    vmem = pl.BlockSpec(memory_space=pltpu.VMEM)
    dma = pltpu.SemaphoreType.DMA
    return pl.pallas_call(
        functools.partial(total_kernel, outer, parts),
        out_shape=jax.ShapeDtypeStruct(one, F32),
        in_specs=[vmem],
        out_specs=vmem,
        scratch_shapes=[
            pltpu.VMEM((outer, PAIR) + one, F32),
            pltpu.VMEM((outer,) + one, F32),
            pltpu.VMEM((outer - 1,) + one, F32),
            pltpu.VMEM((parts,) + one, F32),
            pltpu.VMEM((outer, PAIR) + one, F32),
            pltpu.VMEM((outer,) + one, F32),
            dma, dma, dma, dma, dma((outer,)), dma((outer,)), dma((parts,)), dma((parts,)),
        ],
        compiler_params=pltpu.CompilerParams(collective_id=2, has_side_effects=True),
    )(values)


def local(hidden_acts, down_weight, expert_ids, route_logits, out_grad):
    local_experts, groups, capacity, hidden = hidden_acts.shape
    tok_rows, top_count = expert_ids.shape
    width = out_grad.shape[1]
    parts = lax.axis_size("exp")
    first = lax.axis_index("ctx") * local_experts

    weights = jnp.exp(route_logits)
    route_probs = weights / jnp.sum(weights, axis=1, keepdims=True)

    outer = groups // (PAIR * PAIR)
    routes = gather_routes(
        jnp.concatenate([expert_ids.astype(F32), route_probs], axis=1).T, outer
    ).reshape(groups, 2 * top_count, tok_rows)
    ids = routes[:, :top_count].astype(jnp.int32)
    probs = routes[:, top_count:]

    mine = first + jnp.arange(local_experts, dtype=jnp.int32)
    named = ids[:, None] == mine[None, :, None, None]
    taken = jnp.any(named, axis=2)
    prob_of = jnp.sum(jnp.where(named, probs[:, None], 0.0), axis=2)
    order = jnp.arange(tok_rows)
    earlier = (order[:, None] < order[None, :]).astype(BF16)
    position = jnp.einsum(
        "cet,tu->ceu", taken.astype(BF16), earlier, preferred_element_type=F32
    ).astype(jnp.int32)
    slots = jnp.arange(capacity, dtype=jnp.int32)
    holds = taken[:, :, None, :] & (position[:, :, None, :] == slots[:, None])
    slot_prob = jnp.sum(jnp.where(holds, prob_of[:, :, None, :], 0.0), axis=3)
    select = holds.astype(BF16).reshape(groups, local_experts * capacity, tok_rows)
    back = select.swapaxes(1, 2)

    _, combined, grad_hidden, slot_grad, slot_sum = exchange(
        hidden_acts.reshape(local_experts, groups * capacity, hidden),
        down_weight.swapaxes(1, 2),
        slot_prob[..., None],
        back,
        select,
        out_grad,
        outer,
        parts,
    )
    grad_hidden = grad_hidden.reshape(hidden_acts.shape)
    slot_sum = slot_sum.reshape(local_experts, groups, capacity).swapaxes(0, 1)
    token_sum = jnp.sum(jnp.where(holds, slot_sum[..., None], 0.0), axis=2)
    route_sum = jnp.sum(jnp.where(named, token_sum[:, :, None, :], 0.0), axis=1)
    route_sum = jnp.pad(route_sum, ((0, 0), (0, top_count), (0, 0)))
    route_sum = total_routes(
        route_sum.reshape(outer, PAIR, PAIR, 2 * top_count, tok_rows), outer, parts
    )[:top_count].T
    grad_logits = route_sum - route_probs * jnp.sum(route_sum, axis=1, keepdims=True)
    grad_weight = jnp.einsum(
        "escj,escd->ejd", hidden_acts, slot_grad, preferred_element_type=F32
    ).astype(BF16)
    return (combined, grad_logits, grad_hidden, grad_weight)


def solution(mesh):
    placed = (
        P("ctx", None, None, "exp"),
        P("ctx", "exp", None),
        P("ctx", None),
        P("ctx", None),
        P("ctx", "exp"),
    )
    return jax.shard_map(
        local,
        mesh=mesh,
        in_specs=placed,
        out_specs=(
            P("ctx", "exp"),
            P("ctx", None),
            P("ctx", None, None, "exp"),
            P("ctx", "exp", None),
        ),
        check_vma=False,
    )
```
